128 devices in a mesh: tensor: 8 (over x_hi, y), seq: 16 (over z, x_lo, core).
Axes of the slice: x: 4 (x_hi: 2, x_lo: 2; x = x_hi * 2 + x_lo), y: 4, z: 4, core: 2. Of those that a mesh axis runs over, the one named last changes fastest.
Arguments:
- teacher_query: bfloat16 [6144, 4096], P('seq', 'tensor'), may hold values from -9 to 9
- teacher_keys: bfloat16 [6144, 1024], P('seq', 'tensor'), may hold values from -6 to 6
- teacher_values: bfloat16 [6144, 1024], P('seq', 'tensor'), may hold values from -24 to 24
- out_proj: bfloat16 [4096, 8192], P('tensor'), may hold values from -0.1875 to 0.1875
- teacher_stream: bfloat16 [6144, 8192], P('seq', 'tensor'), may hold values from -6 to 6
- student_stream: bfloat16 [6144, 4096], P('seq', 'tensor'), may hold values from -400 to 400
- student_gain: float32 [4096], replicated, may hold values from 0.25 to 1.75
- distill_proj: bfloat16 [4096, 8192], P('seq', 'tensor'), may hold values from -0.09375 to 0.09375
- token_mask: int32 [6144], P('seq'), may hold values 0 or 1
Outputs:
- grad_distill: bfloat16 [4096, 8192], P('seq', 'tensor')
- grad_stream: float32 [6144, 4096], P('seq', 'tensor')
The draws below stay inside these ranges and needn't reach their ends.
All inputs are finite; a program needn't handle non-finite values. No bound on the sum of `token_mask` on one device may be relied on, other than what follows from the above.
Results may differ from the reference program's by a relative error of at most 0.024.
Values may be sent and summed in bfloat16 or wider, within the bound.
A program may use at most 192 MiB of HBM per device.

```python
import math
import jax
import jax.numpy as jnp
from jax import lax

D_TEACHER = 8192
D_STUDENT = 4096
Q_HEADS = 32
KV_HEADS = 8
HEAD_DIM = 128
TOK_DEV = 384
TOKENS = 6144
N_SEQ = 16


def draw_teacher_query(key, part):
    key = jax.random.fold_in(key, 11)
    drawn = jnp.clip(jax.random.normal(key, (TOKENS, Q_HEADS * HEAD_DIM), jnp.float32), -6.0, 6.0) * 1.5
    return drawn.astype(jnp.bfloat16)


def draw_teacher_keys(key, part):
    key = jax.random.fold_in(key, 17)
    drawn = jnp.clip(jax.random.normal(key, (TOKENS, KV_HEADS * HEAD_DIM), jnp.float32), -6.0, 6.0)
    return drawn.astype(jnp.bfloat16)


def draw_student_stream(key, part):
    key = jax.random.fold_in(key, 23)
    col_key, row_key, base_key = jax.random.split(key, 3)
    columns = jnp.arange(D_STUDENT, dtype=jnp.float32)
    col_scale = jnp.exp(jax.random.uniform(col_key, (D_STUDENT,), jnp.float32, 0.0, math.log(10.0))) * jnp.sqrt(1.0 + 8.0 * columns / D_STUDENT)
    row_scale = jnp.exp(jax.random.uniform(row_key, (TOKENS, 1), jnp.float32, 0.0, math.log(10.0)))
    base = jnp.clip(jax.random.normal(base_key, (TOKENS, D_STUDENT), jnp.float32), -4.0, 4.0)
    return (0.3 * base * row_scale * col_scale).astype(jnp.bfloat16)


def touch_ends(result, own_key, smallest, top_value):
    index_at = [jax.random.randint(jax.random.fold_in(own_key, axis), (), 0, length) for axis, length in enumerate(result.shape)]
    longest = result.shape.index(max(result.shape))
    beside = index_at[:longest] + [(index_at[longest] + 1) % result.shape[longest]] + index_at[longest + 1:]
    return result.at[tuple(index_at)].set(smallest).at[tuple(beside)].set(top_value)


def shard_levels(rng, dims, cuts, smallest, top_value):
    gain = 1.0
    for axis_at, parts in cuts:
        heights = jax.random.uniform(jax.random.fold_in(jax.random.fold_in(rng, 6), axis_at), (parts,), jnp.float32, smallest / len(cuts), top_value / len(cuts))
        gain = gain * jnp.repeat(jnp.exp(heights), dims[axis_at] // parts).reshape((-1,) + (1,) * (len(dims) - 1 - axis_at))
    return gain


def bell_draw(stream_key, extent, spread, most, shards=(), held_as=jnp.bfloat16):
    factor_of = shard_levels(stream_key, extent, shards, -0.22, 0.18) if shards else 1.0
    entries = jax.random.normal(stream_key, extent, jnp.float32) * spread * factor_of
    return jnp.minimum(jnp.maximum(entries, -most), most).astype(held_as)


def setup_inputs(seed: int = 0) -> dict:
    arg_keys = jax.random.split(jax.random.key(seed), 10)
    teacher_query = draw_teacher_query(jax.random.fold_in(arg_keys[9], 71), 0)
    teacher_keys = draw_teacher_keys(jax.random.fold_in(arg_keys[9], 71), 0)
    teacher_values = bell_draw(arg_keys[2], (TOKENS, KV_HEADS * HEAD_DIM), 4.0, 24.0, ((0, 16), (1, 8)))
    out_proj = bell_draw(arg_keys[3], (Q_HEADS * HEAD_DIM, D_TEACHER), (Q_HEADS * HEAD_DIM // 4) ** -0.5, 0.1875, ((0, 8),))
    teacher_stream = bell_draw(arg_keys[4], (TOKENS, D_TEACHER), 1.0, 6.0, ((0, 16), (1, 8)))
    student_stream = draw_student_stream(jax.random.fold_in(arg_keys[9], 71), 0)
    student_gain = jnp.clip(1.0 + 0.15 * jax.random.normal(arg_keys[6], (D_STUDENT,), jnp.float32), 0.25, 1.75)
    distill_proj = bell_draw(arg_keys[7], (D_STUDENT, D_TEACHER), D_STUDENT ** -0.5, 0.09375, ((0, 16), (1, 8)))
    token_mask = touch_ends((jax.random.randint(arg_keys[8], (TOKENS,), 0, 8) < 7).astype(jnp.int32), jax.random.fold_in(arg_keys[8], 1), 0, 1)
    return {"teacher_query": teacher_query, "teacher_keys": teacher_keys, "teacher_values": teacher_values, "out_proj": out_proj, "teacher_stream": teacher_stream, "student_stream": student_stream, "student_gain": student_gain, "distill_proj": distill_proj, "token_mask": token_mask}


masked_score = -1e+30
norm_eps = 1e-05

def attention(teacher_query, teacher_keys, teacher_values):
    group_size = Q_HEADS // KV_HEADS
    score_scale = 1.0 / math.sqrt(HEAD_DIM)
    queries = teacher_query.reshape(TOKENS, Q_HEADS, HEAD_DIM).transpose(1, 0, 2)
    keys_heads = jnp.repeat(teacher_keys.reshape(TOKENS, KV_HEADS, HEAD_DIM).transpose(1, 0, 2), group_size, axis=0)
    values_heads = jnp.repeat(teacher_values.reshape(TOKENS, KV_HEADS, HEAD_DIM).transpose(1, 0, 2), group_size, axis=0)
    positions = jnp.arange(TOKENS, dtype=jnp.int32)
    allowed = positions[:, None] >= positions[None, :]

    def one_head(inputs):
        query_one, keys_one, values_one = inputs
        scores = jnp.dot(query_one, keys_one.T, preferred_element_type=jnp.float32) * score_scale
        scores = jnp.where(allowed, scores, masked_score)
        row_max = lax.optimization_barrier(jnp.max(scores, axis=-1, keepdims=True))
        weights = jnp.where(allowed, jnp.exp(scores - row_max), 0.0)
        totals = lax.optimization_barrier(jnp.sum(weights, axis=-1, keepdims=True))
        mixed = jnp.dot(weights.astype(jnp.bfloat16), values_one, preferred_element_type=jnp.float32)
        return (mixed / totals).astype(jnp.bfloat16)
    context = lax.map(one_head, (queries, keys_heads, values_heads))
    return context.transpose(1, 0, 2).reshape(TOKENS, Q_HEADS * HEAD_DIM)

def reference(teacher_query, teacher_keys, teacher_values, out_proj, teacher_stream, student_stream, student_gain, distill_proj, token_mask):
    context = attention(teacher_query, teacher_keys, teacher_values)
    teacher_out = jnp.dot(context, out_proj, preferred_element_type=jnp.float32)
    target = (teacher_stream.astype(jnp.float32) + teacher_out).astype(jnp.bfloat16)
    hidden = student_stream.astype(jnp.float32)
    inverse = lax.rsqrt(lax.optimization_barrier(jnp.mean(hidden * hidden, axis=-1, keepdims=True)) + norm_eps)
    scaled_rows = hidden * inverse
    normed = (scaled_rows * student_gain).astype(jnp.bfloat16)
    predicted = jnp.dot(normed, distill_proj, preferred_element_type=jnp.float32)
    mismatch = token_mask.astype(jnp.float32)[:, None] * (predicted - target.astype(jnp.float32))
    mismatch_half = mismatch.astype(jnp.bfloat16)
    inv_scale = 1.0 / math.sqrt(TOKENS)

    def group_term(carry_sum, inputs):
        normed_group, mismatch_group = inputs
        term = lax.dot_general(normed_group, mismatch_group, (((0,), (0,)), ((), ())), preferred_element_type=jnp.float32) * inv_scale
        rounded = lax.optimization_barrier(term.astype(jnp.bfloat16))
        return (carry_sum + rounded.astype(jnp.float32), None)
    grad_total, unused = lax.scan(group_term, jnp.zeros((D_STUDENT, D_TEACHER), jnp.float32), (normed.reshape(N_SEQ, TOK_DEV, D_STUDENT), mismatch_half.reshape(N_SEQ, TOK_DEV, D_TEACHER)))
    grad_distill = grad_total.astype(jnp.bfloat16)
    normed_grad = jnp.dot(mismatch_half, distill_proj.T, preferred_element_type=jnp.float32)
    gained = normed_grad * student_gain
    inner_mean = lax.optimization_barrier(jnp.mean(gained * scaled_rows, axis=-1, keepdims=True))
    grad_stream = inverse * (gained - scaled_rows * inner_mean)
    return (grad_distill, grad_stream)
```

```python
import functools
import math

import jax
import jax.numpy as jnp
from jax import lax
from jax.experimental import pallas as pl
from jax.experimental.pallas import tpu as pltpu
from jax.sharding import PartitionSpec as P

HEADS = 4
HEAD_DIM = 128
EPS = 1e-05
ROWS = 384
MASKED = -1e30
MESH = pl.DeviceIdType.MESH
F32 = jnp.float32
BF16 = jnp.bfloat16
SLOTS = 2


def dot(a, b):
    return jnp.dot(a, b, preferred_element_type=F32)


def dot_nt(a, b):
    return lax.dot_general(a, b, (((1,), (1,)), ((), ())), preferred_element_type=F32)


class Copies:
    def __init__(self, send, recv):
        self.send, self.recv = send, recv
        self.started = []

    def make(self, src, dst, k, device):
        return pltpu.make_async_remote_copy(
            src_ref=src, dst_ref=dst, send_sem=self.send.at[k], recv_sem=self.recv.at[k],
            device_id=device, device_id_type=MESH,
        )

    def start(self, src, dst, k, device, again=None):
        self.make(src, dst, k, device).start()
        self.started.append((again or (lambda: src), k, device))

    def arrived(self, ref, k, device):
        self.make(ref, ref, k, device).wait_recv()

    def drain(self):
        for again, k, device in self.started:
            src = again()
            self.make(src, src, k, device).wait_send()
        self.started = []


class Gather:
    def __init__(self, copies, whole, half, near, up, down, ring, pair, other):
        self.c, self.whole, self.half = copies, whole, half
        self.near, self.up, self.down = near, up, down
        self.ring, self.pair, self.other = ring, pair, other

    def at(self, turn, flip):
        r = lax.rem(self.ring + (turn + 4), 4)
        f = 1 - self.pair if flip else self.pair
        return r, f

    def go(self, k, device, place):
        ref = self.whole(*self.at(*place))
        self.c.start(ref, ref, k, device, lambda: self.whole(*self.at(*place)))

    def go_half(self, k, device, place, part):
        ref = self.half(*self.at(*place), part)
        self.c.start(ref, ref, k, device, lambda: self.half(*self.at(*place), part))

    def across(self, k, place):
        if self.other is not None:
            self.go(k, self.other, place)

    def own_near(self):
        self.go(0, self.near, (0, False))

    def own_ring(self):
        self.go(1, self.up, (0, False))
        self.go(2, self.down, (0, False))

    def own_across(self):
        self.across(3, (0, False))

    def got_near(self):
        place = (0, True)
        self.c.arrived(self.whole(*self.at(*place)), 0, self.near)
        self.go(4, self.up, place)
        self.go(5, self.down, place)
        self.across(6, place)

    def got_from_down(self, flip):
        place = (-1, flip)
        self.c.arrived(self.whole(*self.at(*place)), 4 if flip else 1, self.down)
        self.go_half(11 if flip else 7, self.up, place, 0)
        self.across(12 if flip else 8, place)

    def got_from_up(self, flip):
        place = (1, flip)
        self.c.arrived(self.whole(*self.at(*place)), 5 if flip else 2, self.up)
        self.go_half(13 if flip else 9, self.down, place, 1)
        self.across(14 if flip else 10, place)

    def got_far(self, flip):
        place = (2, flip)
        self.c.arrived(self.half(*self.at(*place), 0), 11 if flip else 7, self.down)
        self.c.arrived(self.half(*self.at(*place), 1), 13 if flip else 9, self.up)
        self.across(16 if flip else 15, place)


class Reduce:
    def __init__(self, copies, out, got, near, up, down, ring, pair, base):
        self.c, self.out, self.got = copies, out, got
        self.near, self.up, self.down = near, up, down
        self.ring, self.pair, self.base = ring, pair, base

    def dev(self, k):
        return (self.up, self.down, self.up, self.down, self.up, self.down, self.near)[k]

    def to(self, turn):
        return lax.rem(self.ring + (turn + 4), 4)

    def send(self, j, k, value):
        src = self.out.at[j % SLOTS, k]
        if j >= SLOTS:
            self.c.make(src, src, self.base + (j - SLOTS) * 7 + k, self.dev(k)).wait_send()
        self.out[j % SLOTS, k] = value.astype(BF16)
        self.c.make(src, self.got.at[j, k], self.base + j * 7 + k, self.dev(k)).start()

    def arrived(self, j, k):
        ref = self.got.at[j, k]
        back = (self.down, self.up, self.down, self.up, self.down, self.up, self.near)[k]
        self.c.make(ref, ref, self.base + j * 7 + k, back).wait_recv()

    def load(self, j, k):
        return self.got[j, k].astype(F32)

    def first(self, j, block):
        self.send(j, 0, block(0, self.to(2)))
        self.send(j, 1, block(1, self.to(2)))
        self.send(j, 2, block(1, self.to(1)))
        self.send(j, 3, block(0, self.to(-1)))

    def second(self, j, block):
        self.arrived(j, 0)
        self.send(j, 4, block(0, self.to(1)) + self.load(j, 0))
        self.arrived(j, 1)
        self.send(j, 5, block(1, self.to(-1)) + self.load(j, 1))

    def total(self, j, block, f):
        return block(f, self.ring) + self.load(j, 4 - 2 * f) + self.load(j, 3 + 2 * f)

    def third(self, j, block):
        for k in (2, 3, 4, 5):
            self.arrived(j, k)
        self.send(j, 6, self.total(j, block, 1 - self.pair))

    def last(self, j, block):
        mine = self.total(j, block, self.pair)
        self.arrived(j, 6)
        return mine + self.load(j, 6)

    def drain(self, groups):
        for j in range(max(0, groups - SLOTS), groups):
            for k in range(7):
                src = self.out.at[j % SLOTS, k]
                self.c.make(src, src, self.base + j * 7 + k, self.dev(k)).wait_send()


def kernel(
    q_hbm, k_hbm, v_hbm, op_hbm, ts_ref, ss_hbm, gain_ref, dp_hbm, mask_ref,
    gd_ref, gs_ref,
    q4, kv, dist, stu, normed, normed_t, big, tout, tgot, gout, ggot, sib,
    pred, mm, acc, m_s, l_s, ctx, inv_s, rows_s, ims, imr,
    local, op_sem, kv_s, kv_r, d_s, d_r, s_s, s_r, t_s, t_r, g_s, g_r, b_s, b_r, i_s, i_r,
):
    t, s = lax.axis_index("tensor"), lax.axis_index("seq")
    h, y = lax.div(t, 4), lax.rem(t, 4)
    z, x, c = lax.div(s, 4), lax.rem(lax.div(s, 2), 2), lax.rem(s, 2)
    p = lax.div(s, 2)

    def on_seq(zz, xx, cc):
        return {"tensor": t, "seq": zz * 4 + xx * 2 + cc}

    def on_tensor(hh, yy):
        return {"tensor": hh * 4 + yy, "seq": s}

    z_up, z_down = on_seq(lax.rem(z + 1, 4), x, c), on_seq(lax.rem(z + 3, 4), x, c)
    x_near, sibling = on_seq(z, 1 - x, c), on_seq(z, x, 1 - c)
    y_up, y_down = on_tensor(h, lax.rem(y + 1, 4)), on_tensor(h, lax.rem(y + 3, 4))
    h_near = on_tensor(1 - h, y)

    own_copies = [
        pltpu.make_async_copy(k_hbm, kv.at[0, p, c], local.at[0]),
        pltpu.make_async_copy(v_hbm, kv.at[1, p, c], local.at[1]),
        pltpu.make_async_copy(ss_hbm, stu.at[t], local.at[2]),
        pltpu.make_async_copy(dp_hbm, dist.at[s], local.at[3]),
    ] + [
        pltpu.make_async_copy(q_hbm.at[:, pl.ds(i * HEAD_DIM, HEAD_DIM)], q4.at[i], local.at[4 + i])
        for i in range(HEADS)
    ]
    for copy in own_copies:
        copy.start()

    barrier = pltpu.get_barrier_semaphore()
    for device in (z_up, z_down, x_near, sibling, y_up, y_down, h_near):
        pl.semaphore_signal(barrier, inc=1, device_id=device, device_id_type=MESH)
    pl.semaphore_wait(barrier, 7)

    kv_copies, d_copies, s_copies = Copies(kv_s, kv_r), Copies(d_s, d_r), Copies(s_s, s_r)

    def kv_gather(core):
        return Gather(
            kv_copies, lambda r, f: kv.at[:, r * 2 + f, core], lambda r, f, part: kv.at[part, r * 2 + f, core],
            x_near, z_up, z_down, z, x, sibling,
        )

    def d_gather(core):
        return Gather(
            d_copies, lambda r, f: dist.at[(r * 2 + f) * 2 + core],
            lambda r, f, part: dist.at[(r * 2 + f) * 2 + core, pl.ds(part * 128, 128)],
            x_near, z_up, z_down, z, x, sibling,
        )

    kvg, dg = kv_gather(c), d_gather(c)
    sg = Gather(
        s_copies, lambda r, f: stu.at[f * 4 + r],
        lambda r, f, part: stu.at[f * 4 + r, pl.ds(part * 192, 192)],
        h_near, y_up, y_down, y, h, None,
    )

    def from_sibling(gather, copies, k, turn, flip):
        copies.arrived(gather.whole(*gather.at(turn, flip)), k, sibling)

    kv_other, d_other = kv_gather(1 - c), d_gather(1 - c)

    own_copies[0].wait()
    own_copies[1].wait()
    kvg.own_across()
    kvg.own_near()
    kvg.own_ring()
    own_copies[2].wait()
    sg.own_ring()
    own_copies[3].wait()
    for copy in own_copies[4:]:
        copy.wait()

    def load_out_proj(i, carry):
        for j in range(4):
            start = pl.multiple_of(i * 1024 + j * 256, 256)
            for half in range(2):
                pltpu.make_async_copy(
                    op_hbm.at[pl.ds(half * 256, 256), pl.ds(start, 256)], big.at[j, i, half], op_sem.at[j, i, half]
                ).start()
        return carry

    lax.fori_loop(0, 8, load_out_proj, 0)

    scale = math.log2(math.e) / math.sqrt(HEAD_DIM)

    from_sibling(kv_other, kv_copies, 3, 0, False)
    kk0, vv0 = kv[0, p].reshape(2 * ROWS, HEAD_DIM), kv[1, p].reshape(2 * ROWS, HEAD_DIM)
    visible = (
        lax.broadcasted_iota(jnp.int32, (ROWS, 2 * ROWS), 1)
        <= lax.broadcasted_iota(jnp.int32, (ROWS, 2 * ROWS), 0) + c * ROWS
    )
    for i in range(HEADS):
        scores = jnp.where(visible, dot_nt(q4[i], kk0) * scale, MASKED)
        top = jnp.max(scores, axis=1, keepdims=True)
        weights = jnp.exp2(scores - top)
        m_s[i] = jnp.broadcast_to(top, (ROWS, 128))
        l_s[i] = jnp.broadcast_to(jnp.sum(weights, axis=1, keepdims=True), (ROWS, 128))
        acc[i] = dot(weights.astype(BF16), vv0)

    def step(i, carry):
        @pl.when(i == 1)
        def _():
            kvg.got_near()
            kvg.got_from_down(False)
            kvg.got_from_up(False)
            sg.own_near()
            from_sibling(kv_other, kv_copies, 6, 0, True)

        @pl.when(i == 2)
        def _():
            from_sibling(kv_other, kv_copies, 8, -1, False)
            dg.own_across()
            dg.own_near()
            dg.own_ring()

        @pl.when(i == 3)
        def _():
            from_sibling(kv_other, kv_copies, 10, 1, False)

        @pl.when(i == 4)
        def _():
            kvg.got_from_down(True)
            kvg.got_from_up(True)
            kvg.got_far(False)
            from_sibling(kv_other, kv_copies, 15, 2, False)

        @pl.when(i == 5)
        def _():
            sg.got_near()
            from_sibling(kv_other, kv_copies, 12, -1, True)

        @pl.when(i == 6)
        def _():
            from_sibling(kv_other, kv_copies, 14, 1, True)

        @pl.when(i == 7)
        def _():
            kvg.got_far(True)
            from_sibling(kv_other, kv_copies, 16, 2, True)

        turn = jnp.where(i == 1, 0, jnp.where((i == 2) | (i == 5), 3, jnp.where((i == 3) | (i == 6), 1, 2)))
        flip = jnp.where((i == 1) | (i >= 5), 1 - x, x)
        block = lax.rem(z + turn, 4) * 2 + flip

        @pl.when(block < p)
        def _():
            kk, vv = kv[0, block].reshape(2 * ROWS, HEAD_DIM), kv[1, block].reshape(2 * ROWS, HEAD_DIM)
            for i in range(HEADS):
                scores = dot_nt(q4[i], kk)
                before = m_s[i, :, 0:1]
                top = jnp.maximum(before, jnp.max(scores, axis=1, keepdims=True) * scale)
                weights = jnp.exp2(scores * scale - top)
                fade = jnp.exp2(before - top)
                m_s[i] = jnp.broadcast_to(top, (ROWS, 128))
                l_s[i] = l_s[i] * fade + jnp.sum(weights, axis=1, keepdims=True)
                acc[i] = acc[i] * fade + dot(weights.astype(BF16), vv)

        return carry

    lax.fori_loop(1, 8, step, 0)

    for i in range(HEADS):
        ctx[:, i * HEAD_DIM : (i + 1) * HEAD_DIM] = (acc[i] / l_s[i]).astype(BF16)

    t_copies, g_copies = Copies(t_s, t_r), Copies(g_s, g_r)
    tr = Reduce(t_copies, tout, tgot, h_near, y_up, y_down, y, h, 0)
    gr = Reduce(g_copies, gout, ggot, x_near, z_up, z_down, z, x, 0)

    def out_block(j):
        return lambda f, r: dot(ctx[...], big[j, f * 4 + r].reshape(512, 256))

    def out_proj_here(j):
        def wait(i, carry):
            start = pl.multiple_of(i * 1024 + j * 256, 256)
            for half in range(2):
                pltpu.make_async_copy(
                    op_hbm.at[pl.ds(half * 256, 256), pl.ds(start, 256)], big.at[j, i, half], op_sem.at[j, i, half]
                ).wait()
            return carry

        lax.fori_loop(0, 8, wait, 0)

    for j in range(4):
        out_proj_here(j)

    tr.first(0, out_block(0))
    sg.got_from_down(False)
    sg.got_from_up(False)
    dg.got_near()
    dg.got_from_down(False)
    dg.got_from_up(False)
    sg.got_from_down(True)
    sg.got_from_up(True)
    tr.first(1, out_block(1))
    tr.second(0, out_block(0))
    sg.got_far(False)
    sg.got_far(True)

    def squares(i, total):
        block = stu[i].astype(F32)
        block = block * block
        return total + block[:, 0:128] + block[:, 128:256] + block[:, 256:384] + block[:, 384:512]

    square_sum = lax.fori_loop(0, 8, squares, jnp.zeros((ROWS, 128), F32))
    inverse = lax.rsqrt(jnp.sum(square_sum, axis=1, keepdims=True) * (1.0 / 4096) + EPS)
    inv_s[...] = jnp.broadcast_to(inverse, (ROWS, 128))

    def make_normed(i, carry):
        column = pl.multiple_of(i * 512, 512)
        rows = (stu[i].astype(F32) * inv_s[:, 0:1]) * gain_ref[:, pl.ds(column, 512)]
        normed[:, pl.ds(column, 512)] = rows.astype(BF16)
        normed_t[i, 0] = rows[:, 0:256].T.astype(BF16)
        normed_t[i, 1] = rows[:, 256:512].T.astype(BF16)
        return carry

    lax.fori_loop(0, 8, make_normed, 0)

    dg.got_from_down(True)
    dg.got_from_up(True)
    dg.got_far(False)
    tr.first(2, out_block(2))
    tr.third(0, out_block(0))
    tr.second(1, out_block(1))
    dg.got_far(True)
    for k, turn, flip in ((3, 0, 0), (6, 0, 1), (8, -1, 0), (10, 1, 0), (12, -1, 1), (14, 1, 1), (15, 2, 0), (16, 2, 1)):
        from_sibling(d_other, d_copies, k, turn, flip)

    def predict(j, carry):
        pred[j] = dot(normed[...], dist[:, :, pl.ds(pl.multiple_of(j * 256, 256), 256)].reshape(4096, 256))
        return carry

    lax.fori_loop(0, 4, predict, 0)

    inv_scale = 1.0 / math.sqrt(16 * ROWS)

    def mismatch(j):
        teacher = tr.last(j, out_block(j))
        target = (ts_ref[:, j * 256 : (j + 1) * 256].astype(F32) + teacher).astype(BF16).astype(F32)
        half = (mask_ref[...] * (pred[j] - target)).astype(BF16)
        mm[:, j * 256 : (j + 1) * 256] = half
        product = half.astype(F32) * pred[j]
        rows = product[:, 0:128] + product[:, 128:256]
        rows_s[...] = rows if j == 0 else rows_s[...] + rows

    def grad_terms(j):
        mine = mm[:, j * 256 : (j + 1) * 256]

        def term(core):
            def one(i, carry):
                big[j, i, core] = (dot(normed_t[i, core], mine) * inv_scale).astype(BF16)
                return carry

            lax.fori_loop(0, 8, one, 0)

        term(1 - c)
        src = big.at[j, :, 1 - c]
        pltpu.make_async_remote_copy(
            src_ref=src, dst_ref=sib.at[j], send_sem=b_s.at[j], recv_sem=b_r.at[j],
            device_id=sibling, device_id_type=MESH,
        ).start()
        term(c)

    def sibling_done(j, send):
        src = big.at[j, :, 1 - c]
        copy = pltpu.make_async_remote_copy(
            src_ref=src, dst_ref=sib.at[j], send_sem=b_s.at[j], recv_sem=b_r.at[j],
            device_id=sibling, device_id_type=MESH,
        )
        if send:
            copy.wait_send()
        else:
            copy.wait_recv()

    def grad_block(j):
        return lambda f, r: big[j, r * 2 + f, c].astype(F32) + sib[j, r * 2 + f].astype(F32)

    def grad_last(j):
        gd_ref[:, j * 256 : (j + 1) * 256] = gr.last(j, grad_block(j)).astype(BF16)

    def grad_first(j):
        grad_terms(j)
        sibling_done(j, False)
        gr.first(j, grad_block(j))

    mismatch(0)
    grad_first(0)
    tr.first(3, out_block(3))
    tr.third(1, out_block(1))
    tr.second(2, out_block(2))
    gr.second(0, grad_block(0))
    mismatch(1)
    grad_first(1)
    tr.third(2, out_block(2))
    tr.second(3, out_block(3))
    gr.third(0, grad_block(0))
    gr.second(1, grad_block(1))
    mismatch(2)
    grad_first(2)
    tr.third(3, out_block(3))
    grad_last(0)
    gr.third(1, grad_block(1))
    gr.second(2, grad_block(2))
    mismatch(3)

    def norm_block(j):
        return lambda f, r: dot_nt(mm[...], dist[(f * 4 + r) * 2 + (j - 4)])

    i_copies = Copies(i_s, i_r)
    tr.first(4, norm_block(4))
    row_sum = jnp.broadcast_to(jnp.sum(rows_s[...], axis=1, keepdims=True), (ROWS, 128)).T[0:8]
    ims[0] = row_sum
    i_copies.start(ims.at[0], imr.at[0], 0, h_near)
    grad_first(3)
    i_copies.arrived(imr.at[0], 0, h_near)
    ims[1] = ims[0] + imr[0]
    i_copies.start(ims.at[1], imr.at[1], 1, y_up)
    i_copies.start(ims.at[1], imr.at[2], 2, y_down)
    tr.first(5, norm_block(5))
    tr.second(4, norm_block(4))
    i_copies.arrived(imr.at[1], 1, y_down)
    i_copies.arrived(imr.at[2], 2, y_up)
    i_copies.start(imr.at[1], imr.at[3], 3, y_up)
    grad_last(1)
    gr.third(2, grad_block(2))
    gr.second(3, grad_block(3))
    tr.second(5, norm_block(5))
    tr.third(4, norm_block(4))
    grad_last(2)
    gr.third(3, grad_block(3))
    i_copies.arrived(imr.at[3], 3, y_down)
    total = ims[1] + imr[1] + imr[2] + imr[3]
    inner = jnp.broadcast_to(total[0:1], (128, ROWS)).T[:, 0:1] * (1.0 / 4096)

    def stream_grad(j):
        g = j - 4
        column = pl.multiple_of(t * 512 + g * 256, 256)
        gained = tr.last(j, norm_block(j)) * gain_ref[:, pl.ds(column, 256)]
        inv = inv_s[:, 0:1]
        scaled = stu[t, :, g * 256 : (g + 1) * 256].astype(F32) * inv
        gs_ref[:, g * 256 : (g + 1) * 256] = inv * (gained - scaled * inner)

    grad_last(3)
    tr.third(5, norm_block(5))
    stream_grad(4)
    stream_grad(5)

    for copies in (kv_copies, d_copies, s_copies, i_copies):
        copies.drain()
    for j in range(4):
        sibling_done(j, True)
    tr.drain(6)
    gr.drain(4)


def body(q, k, v, out_proj, teacher_stream, student_stream, gain, distill, mask):
    anywhere = pl.BlockSpec(memory_space=pl.ANY)
    vmem = pl.BlockSpec(memory_space=pltpu.VMEM)
    sem = pltpu.SemaphoreType.DMA
    return pl.pallas_call(
        kernel,
        out_shape=(jax.ShapeDtypeStruct((256, 1024), BF16), jax.ShapeDtypeStruct((ROWS, 512), F32)),
        in_specs=[anywhere] * 4 + [vmem, anywhere, vmem, anywhere, vmem],
        out_specs=(vmem, vmem),
        scratch_shapes=[
            pltpu.VMEM((HEADS, ROWS, HEAD_DIM), BF16),
            pltpu.VMEM((2, 8, 2, ROWS, HEAD_DIM), BF16),
            pltpu.VMEM((16, 256, 1024), BF16),
            pltpu.VMEM((8, ROWS, 512), BF16),
            pltpu.VMEM((ROWS, 4096), BF16),
            pltpu.VMEM((8, 2, 256, ROWS), BF16),
            pltpu.VMEM((4, 8, 2, 256, 256), BF16),
            pltpu.VMEM((SLOTS, 7, ROWS, 256), BF16),
            pltpu.VMEM((6, 7, ROWS, 256), BF16),
            pltpu.VMEM((SLOTS, 7, 256, 256), BF16),
            pltpu.VMEM((4, 7, 256, 256), BF16),
            pltpu.VMEM((4, 8, 256, 256), BF16),
            pltpu.VMEM((4, ROWS, 256), F32),
            pltpu.VMEM((ROWS, 1024), BF16),
            pltpu.VMEM((HEADS, ROWS, HEAD_DIM), F32),
            pltpu.VMEM((HEADS, ROWS, 128), F32),
            pltpu.VMEM((HEADS, ROWS, 128), F32),
            pltpu.VMEM((ROWS, 512), BF16),
            pltpu.VMEM((ROWS, 128), F32),
            pltpu.VMEM((ROWS, 128), F32),
            pltpu.VMEM((2, 8, ROWS), F32),
            pltpu.VMEM((4, 8, ROWS), F32),
            sem((8,)), sem((4, 8, 2)),
            sem((17,)), sem((17,)), sem((17,)), sem((17,)), sem((17,)), sem((17,)),
            sem((42,)), sem((42,)), sem((28,)), sem((28,)), sem((4,)), sem((4,)), sem((4,)), sem((4,)),
        ],
        compiler_params=pltpu.CompilerParams(
            collective_id=0, has_side_effects=True, vmem_limit_bytes=63 * 2**20
        ),
        name="distill",
    )(
        q, k, v, out_proj, teacher_stream, student_stream, gain.reshape(1, 4096), distill,
        mask.astype(F32).reshape(ROWS, 1),
    )


def solution(mesh):
    placed = (
        P("seq", "tensor"),
        P("seq", "tensor"),
        P("seq", "tensor"),
        P("tensor", None),
        P("seq", "tensor"),
        P("seq", "tensor"),
        P(),
        P("seq", "tensor"),
        P("seq"),
    )
    return jax.shard_map(
        body,
        mesh=mesh,
        in_specs=placed,
        out_specs=(P("seq", "tensor"), P("seq", "tensor")),
        check_vma=False,
    )
```

```python
import functools
import math

import jax
import jax.numpy as jnp
from jax import lax
from jax.experimental import pallas as pl
from jax.experimental.pallas import tpu as pltpu
from jax.sharding import PartitionSpec as P

HEADS = 4
HEAD_DIM = 128
EPS = 1e-05
ROWS = 384
MASKED = -1e30
MESH = pl.DeviceIdType.MESH
F32 = jnp.float32
BF16 = jnp.bfloat16


def dot(a, b):
    return jnp.dot(a, b, preferred_element_type=F32)


def dot_nt(a, b):
    return lax.dot_general(a, b, (((1,), (1,)), ((), ())), preferred_element_type=F32)


PAIR_FIRST_T = (2, 3, 5)
PAIR_FIRST_G = ()


class Copies:
    def __init__(self, send, recv):
        self.send, self.recv = send, recv
        self.started = []

    def make(self, src, dst, k, device):
        return pltpu.make_async_remote_copy(
            src_ref=src, dst_ref=dst, send_sem=self.send.at[k], recv_sem=self.recv.at[k],
            device_id=device, device_id_type=MESH,
        )

    def start(self, src, dst, k, device, again=None):
        self.make(src, dst, k, device).start()
        self.started.append((again or (lambda: src), k, device))

    def arrived(self, ref, k, device):
        self.make(ref, ref, k, device).wait_recv()

    def drain(self):
        for again, k, device in self.started:
            src = again()
            self.make(src, src, k, device).wait_send()
        self.started = []


class Gather:
    def __init__(self, copies, whole, half, near, up, down, ring, pair, other):
        self.c, self.whole, self.half = copies, whole, half
        self.near, self.up, self.down = near, up, down
        self.ring, self.pair, self.other = ring, pair, other
        self.loads = []

    def loaded(self):
        for copy in self.loads:
            copy.wait()
        self.loads = []

    def at(self, turn, flip):
        r = lax.rem(self.ring + (turn + 4), 4)
        f = 1 - self.pair if flip else self.pair
        return r, f

    def go(self, k, device, place):
        ref = self.whole(*self.at(*place))
        self.c.start(ref, ref, k, device, lambda: self.whole(*self.at(*place)))

    def go_half(self, k, device, place, part):
        ref = self.half(*self.at(*place), part)
        self.c.start(ref, ref, k, device, lambda: self.half(*self.at(*place), part))

    def across(self, k, place):
        if self.other is not None:
            self.go(k, self.other, place)

    def own_near(self):
        self.loaded()
        self.go(0, self.near, (0, False))

    def own_ring(self):
        self.loaded()
        self.go(1, self.up, (0, False))
        self.go(2, self.down, (0, False))

    def own_across(self):
        self.loaded()
        self.across(3, (0, False))

    def got_near(self):
        place = (0, True)
        self.c.arrived(self.whole(*self.at(*place)), 0, self.near)
        self.go(4, self.up, place)
        self.go(5, self.down, place)
        self.across(6, place)

    def got_from_down(self, flip):
        place = (-1, flip)
        self.c.arrived(self.whole(*self.at(*place)), 4 if flip else 1, self.down)
        self.go_half(11 if flip else 7, self.up, place, 0)
        self.across(12 if flip else 8, place)

    def got_from_up(self, flip):
        place = (1, flip)
        self.c.arrived(self.whole(*self.at(*place)), 5 if flip else 2, self.up)
        self.go_half(13 if flip else 9, self.down, place, 1)
        self.across(14 if flip else 10, place)

    def got_far(self, flip):
        place = (2, flip)
        self.c.arrived(self.half(*self.at(*place), 0), 11 if flip else 7, self.down)
        self.c.arrived(self.half(*self.at(*place), 1), 13 if flip else 9, self.up)
        self.across(16 if flip else 15, place)

    def down_own(self):
        self.got_from_down(False)

    def down_pair(self):
        self.got_from_down(True)

    def up_own(self):
        self.got_from_up(False)

    def up_pair(self):
        self.got_from_up(True)

    def far_own(self):
        self.got_far(False)

    def far_pair(self):
        self.got_far(True)


class Reduce:
    def __init__(self, copies, out, got, near, up, down, ring, pair, places):
        self.c, self.out, self.got = copies, out, got
        self.near, self.up, self.down = near, up, down
        self.ring, self.pair, self.places = ring, pair, places
        self.half = out.shape[2] // 2
        self.pending = {}

    def to(self, turn):
        return lax.rem(self.ring + (turn + 4), 4)

    def put(self, j, slot, value):
        o = self.places[j]
        for src, sem, device in self.pending.pop((o, slot), []):
            self.c.make(src, src, sem, device).wait_send()
        self.out[o, slot] = value.astype(BF16)

    def post(self, j, slot, k, device, part=None):
        rows = slice(None) if part is None else pl.ds(part * self.half, self.half)
        o, sem = self.places[j], j * 8 + k
        src = self.out.at[o, slot, rows]
        self.c.make(src, self.got.at[j, slot, rows], sem, device).start()
        self.pending.setdefault((o, slot), []).append((src, sem, device))

    def send(self, j, k, device, value):
        self.put(j, k, value)
        self.post(j, k, k, device)

    def arrived(self, j, slot, k, device, part=None):
        rows = slice(None) if part is None else pl.ds(part * self.half, self.half)
        ref = self.got.at[j, slot, rows]
        self.c.make(ref, ref, j * 8 + k, device).wait_recv()

    def load(self, j, k):
        return self.got[j, k].astype(F32)


    def first(self, j, block):
        self.send(j, 0, self.up, block(0, self.to(2)))
        self.send(j, 1, self.down, block(1, self.to(2)))
        self.send(j, 2, self.up, block(1, self.to(1)))
        self.send(j, 3, self.down, block(0, self.to(-1)))

    def second(self, j, block):
        self.arrived(j, 0, 0, self.down)
        self.send(j, 4, self.up, block(0, self.to(1)) + self.load(j, 0))
        self.arrived(j, 1, 1, self.up)
        self.send(j, 5, self.down, block(1, self.to(-1)) + self.load(j, 1))

    def total(self, j, block, f):
        return block(f, self.ring) + self.load(j, 4 - 2 * f) + self.load(j, 3 + 2 * f)

    def third(self, j, block):
        for k, device in ((2, self.down), (3, self.up), (4, self.down), (5, self.up)):
            self.arrived(j, k, k, device)
        self.send(j, 6, self.near, self.total(j, block, 1 - self.pair))

    def last(self, j, block):
        mine = self.total(j, block, self.pair)
        self.arrived(j, 6, 6, self.near)
        return mine + self.load(j, 6)


    def near_first(self, j, block):
        for r in range(4):
            self.send(j, r, self.near, block(1 - self.pair, r))

    def both(self, j, block, r):
        return block(self.pair, r) + self.load(j, r)

    def near_ring(self, j, block):
        for r in range(4):
            self.arrived(j, r, r, self.near)
        self.put(j, 4, self.both(j, block, self.to(2)))
        self.post(j, 4, 4, self.up, 0)
        self.post(j, 4, 5, self.down, 1)

    def near_second(self, j, block):
        o, n = self.places[j], self.half
        value = self.both(j, block, self.to(1))
        self.arrived(j, 4, 4, self.down, 0)
        self.put(j, 5, value)
        self.out[o, 5, 0:n] = (value[0:n] + self.got[j, 4, 0:n].astype(F32)).astype(BF16)
        self.post(j, 5, 6, self.up)
        value = self.both(j, block, self.to(-1))
        self.arrived(j, 4, 5, self.up, 1)
        self.put(j, 6, value)
        self.out[o, 6, n : 2 * n] = (value[n : 2 * n] + self.got[j, 4, n : 2 * n].astype(F32)).astype(BF16)
        self.post(j, 6, 7, self.down)

    def near_last(self, j, block):
        mine = self.both(j, block, self.ring)
        self.arrived(j, 5, 6, self.down)
        self.arrived(j, 6, 7, self.up)
        return mine + self.load(j, 5) + self.load(j, 6)

    def drain(self):
        for sent in self.pending.values():
            for src, sem, device in sent:
                self.c.make(src, src, sem, device).wait_send()
        self.pending = {}


class Group:
    def __init__(self, reduce, j, block, ready):
        self.reduce, self.j, self.block, self.ready = reduce, j, block, ready

    def first(self):
        if self.ready is not None:
            self.ready()
        self.reduce.first(self.j, self.block)

    def near_first(self):
        if self.ready is not None:
            self.ready()
        self.reduce.near_first(self.j, self.block)

    def second(self):
        self.reduce.second(self.j, self.block)

    def third(self):
        self.reduce.third(self.j, self.block)

    def near_ring(self):
        self.reduce.near_ring(self.j, self.block)

    def near_second(self):
        self.reduce.near_second(self.j, self.block)


def kernel(
    q_hbm, k_hbm, v_hbm, op_hbm, ts_hbm, ss_hbm, gain_ref, dp_hbm, mask_ref,
    gd_ref, gs_ref,
    q4, kv, dist, stu, normed, normed_t, big, tout, tgot, gout, ggot, sib,
    pred, mm, ts_ref, mask_s, acc, m_s, ctx, inv_s, rows_s, inner_s, ims, imr,
    local, op_sem, kv_s, kv_r, d_s, d_r, s_s, s_r, t_s, t_r, g_s, g_r, b_s, b_r, i_s, i_r,
):
    me, s = lax.axis_index("tensor"), lax.axis_index("seq")
    h, y = lax.div(me, 4), lax.rem(me, 4)
    z, x, c = lax.div(s, 4), lax.rem(lax.div(s, 2), 2), lax.rem(s, 2)
    p = lax.div(s, 2)

    def on_seq(zz, xx, cc):
        return {"tensor": me, "seq": zz * 4 + xx * 2 + cc}

    def on_tensor(hh, yy):
        return {"tensor": hh * 4 + yy, "seq": s}

    z_up, z_down = on_seq(lax.rem(z + 1, 4), x, c), on_seq(lax.rem(z + 3, 4), x, c)
    x_near, sibling = on_seq(z, 1 - x, c), on_seq(z, x, 1 - c)
    y_up, y_down = on_tensor(h, lax.rem(y + 1, 4)), on_tensor(h, lax.rem(y + 3, 4))
    h_near = on_tensor(1 - h, y)

    own_copies = [
        pltpu.make_async_copy(k_hbm, kv.at[0, p, c], local.at[0]),
        pltpu.make_async_copy(v_hbm, kv.at[1, p, c], local.at[1]),
        pltpu.make_async_copy(ss_hbm, stu.at[me], local.at[2]),
        pltpu.make_async_copy(dp_hbm, dist.at[s], local.at[3]),
    ] + [
        pltpu.make_async_copy(q_hbm.at[:, pl.ds(i * HEAD_DIM, HEAD_DIM)], q4.at[i], local.at[4 + i])
        for i in range(HEADS)
    ]
    for copy in own_copies:
        copy.start()

    barrier = pltpu.get_barrier_semaphore()
    for device in (z_up, z_down, x_near, sibling, y_up, y_down, h_near):
        pl.semaphore_signal(barrier, inc=1, device_id=device, device_id_type=MESH)
    pl.semaphore_wait(barrier, 7)

    kv_copies, d_copies, s_copies = Copies(kv_s, kv_r), Copies(d_s, d_r), Copies(s_s, s_r)

    def kv_gather(core):
        return Gather(
            kv_copies, lambda r, f: kv.at[:, r * 2 + f, core], lambda r, f, part: kv.at[part, r * 2 + f, core],
            x_near, z_up, z_down, z, x, sibling,
        )

    def d_gather(core):
        return Gather(
            d_copies, lambda r, f: dist.at[(r * 2 + f) * 2 + core],
            lambda r, f, part: dist.at[(r * 2 + f) * 2 + core, pl.ds(part * 128, 128)],
            x_near, z_up, z_down, z, x, sibling,
        )

    kvg, dg = kv_gather(c), d_gather(c)
    sg = Gather(
        s_copies, lambda r, f: stu.at[f * 4 + r],
        lambda r, f, part: stu.at[f * 4 + r, pl.ds(part * 192, 192)],
        h_near, y_up, y_down, y, h, None,
    )

    def from_sibling(gather, copies, k, turn, flip):
        copies.arrived(gather.whole(*gather.at(turn, flip)), k, sibling)

    kv_other, d_other = kv_gather(1 - c), d_gather(1 - c)

    kvg.loads, sg.loads, dg.loads = own_copies[0:2], own_copies[2:3], own_copies[3:4]

    def load_out_proj(i, carry):
        for j in range(4):
            start = pl.multiple_of(i * 1024 + j * 256, 256)
            for half in range(2):
                pltpu.make_async_copy(
                    op_hbm.at[pl.ds(half * 256, 256), pl.ds(start, 256)], big.at[j, i, half], op_sem.at[j, i, half]
                ).start()
        return carry

    load_stream = pltpu.make_async_copy(ts_hbm, ts_ref, local.at[8])

    def load_later():
        lax.fori_loop(0, 8, load_out_proj, 0)
        load_stream.start()
        rows_s[...] = jnp.zeros_like(rows_s)

    scale = math.log2(math.e) / math.sqrt(HEAD_DIM)

    ones = jnp.ones((2 * ROWS, HEAD_DIM), BF16)

    def keys_values(block):
        values = kv[1, block].reshape(2 * ROWS, HEAD_DIM)
        return kv[0, block].reshape(2 * ROWS, HEAD_DIM), jnp.concatenate([values, ones], axis=1)

    def own_pair():
        load_later()
        for copy in own_copies[4:]:
            copy.wait()
        from_sibling(kv_other, kv_copies, 3, 0, False)
        keys, values = keys_values(p)
        visible = (
            lax.broadcasted_iota(jnp.int32, (ROWS, 2 * ROWS), 1)
            <= lax.broadcasted_iota(jnp.int32, (ROWS, 2 * ROWS), 0) + c * ROWS
        )
        scores = dot_nt(q4[0], keys)
        for i in range(HEADS):
            following = dot_nt(q4[i + 1], keys) if i + 1 < HEADS else None
            scores = jnp.where(visible, scores * scale, MASKED)
            top = jnp.max(scores, axis=1, keepdims=True)
            weights = jnp.exp2(scores - top)
            m_s[i] = jnp.broadcast_to(top, (ROWS, 128))
            acc[i] = dot(weights.astype(BF16), values)
            scores = following

    def step(i, carry):
        turn, flip = 0, 0
        for k, (tasks, (copy, turn_k, flip_k)) in enumerate(attended):
            @pl.when(i == k)
            def _(tasks=tasks, copy=copy, turn_k=turn_k, flip_k=flip_k):
                for task in tasks:
                    task()
                from_sibling(kv_other, kv_copies, copy, turn_k, flip_k)

            turn = jnp.where(i == k, turn_k % 4, turn)
            flip = jnp.where(i == k, int(flip_k), flip)
        block = lax.rem(z + turn, 4) * 2 + x * (1 - flip) + (1 - x) * flip

        @pl.when(block < p)
        def _():
            keys, values = keys_values(block)
            scores = dot_nt(q4[0], keys)
            for i in range(HEADS):
                following = dot_nt(q4[i + 1], keys) if i + 1 < HEADS else None
                before = m_s[i, :, 0:1]
                top = jnp.maximum(before, jnp.max(scores, axis=1, keepdims=True) * scale)
                weights = jnp.exp2(scores * scale - top)
                m_s[i] = jnp.broadcast_to(top, (ROWS, 128))
                acc[i] = acc[i] * jnp.exp2(before - top) + dot(weights.astype(BF16), values)
                scores = following

        return carry

    t_copies, g_copies = Copies(t_s, t_r), Copies(g_s, g_r)
    tr = Reduce(t_copies, tout, tgot, h_near, y_up, y_down, y, h, (0, 1, 2, 0, 1, 2))
    gr = Reduce(g_copies, gout, ggot, x_near, z_up, z_down, z, x, (0, 1, 0, 1))

    def out_block(j):
        return lambda f, r: dot(ctx[...], big[j, f * 4 + r].reshape(512, 256))

    def out_proj_here(j):
        def wait(i, carry):
            start = pl.multiple_of(i * 1024 + j * 256, 256)
            for half in range(2):
                pltpu.make_async_copy(
                    op_hbm.at[pl.ds(half * 256, 256), pl.ds(start, 256)], big.at[j, i, half], op_sem.at[j, i, half]
                ).wait()
            return carry

        lax.fori_loop(0, 8, wait, 0)

    def finish_context():
        for i in range(HEADS):
            ctx[:, i * HEAD_DIM : (i + 1) * HEAD_DIM] = (acc[i, :, 0:HEAD_DIM] / acc[i, :, HEAD_DIM:]).astype(BF16)
        for j in range(4):
            out_proj_here(j)
        load_stream.wait()
        for i in range(3):
            row = mask_ref[i : i + 1, :].astype(F32)
            mask_s[i * 128 : (i + 1) * 128, :] = jnp.broadcast_to(row, (128, 128)).T

    def squares(i, total):
        block = stu[i].astype(F32)
        block = block * block
        return total + block[:, 0:128] + block[:, 128:256] + block[:, 256:384] + block[:, 384:512]

    def make_normed(i, carry):
        column = pl.multiple_of(i * 512, 512)
        rows = (stu[i].astype(F32) * inv_s[:, 0:1]) * gain_ref[:, pl.ds(column, 512)]
        normed[:, pl.ds(column, 512)] = rows.astype(BF16)
        normed_t[i, 0] = rows[:, 0:256].T.astype(BF16)
        normed_t[i, 1] = rows[:, 256:512].T.astype(BF16)
        return carry

    def normalise():
        square_sum = lax.fori_loop(0, 8, squares, jnp.zeros((ROWS, 128), F32))
        inverse = lax.rsqrt(jnp.sum(square_sum, axis=1, keepdims=True) * (1.0 / 4096) + EPS)
        inv_s[...] = jnp.broadcast_to(inverse, (ROWS, 128))
        lax.fori_loop(0, 8, make_normed, 0)

    def predict(j, carry):
        pred[j] = dot(normed[...], dist[:, :, pl.ds(pl.multiple_of(j * 256, 256), 256)].reshape(4096, 256))
        return carry

    def predict_all():
        for k, turn, flip in (
            (3, 0, 0), (6, 0, 1), (8, -1, 0), (10, 1, 0), (12, -1, 1), (14, 1, 1), (15, 2, 0), (16, 2, 1)
        ):
            from_sibling(d_other, d_copies, k, turn, flip)
        lax.fori_loop(0, 4, predict, 0)

    inv_scale = 1.0 / math.sqrt(16 * ROWS)

    def mismatch(j):
        teacher = (tr.near_last if j in PAIR_FIRST_T else tr.last)(j, out_block(j))
        target = (ts_ref[:, j * 256 : (j + 1) * 256].astype(F32) + teacher).astype(BF16).astype(F32)
        half = (mask_s[:, 0:1] * (pred[j] - target)).astype(BF16)
        mm[:, j * 256 : (j + 1) * 256] = half
        product = half.astype(F32) * pred[j]
        rows = product[:, 0:128] + product[:, 128:256]
        rows_s[...] = rows_s[...] + rows

    def grad_terms(j):
        mine = mm[:, j * 256 : (j + 1) * 256]

        def term(core):
            rows = normed_t[:, core].reshape(2048, ROWS)
            big[j, :, core] = (dot(rows, mine) * inv_scale).astype(BF16).reshape(8, 256, 256)

        term(1 - c)
        src = big.at[j, :, 1 - c]
        pltpu.make_async_remote_copy(
            src_ref=src, dst_ref=sib.at[j], send_sem=b_s.at[j], recv_sem=b_r.at[j],
            device_id=sibling, device_id_type=MESH,
        ).start()
        term(c)

    def sibling_done(j, send):
        src = big.at[j, :, 1 - c]
        copy = pltpu.make_async_remote_copy(
            src_ref=src, dst_ref=sib.at[j], send_sem=b_s.at[j], recv_sem=b_r.at[j],
            device_id=sibling, device_id_type=MESH,
        )
        if send:
            copy.wait_send()
        else:
            copy.wait_recv()

    def grad_block(j):
        return lambda f, r: big[j, r * 2 + f, c].astype(F32) + sib[j, r * 2 + f].astype(F32)

    def grad_last(j):
        last = gr.near_last if j in PAIR_FIRST_G else gr.last
        gd_ref[:, j * 256 : (j + 1) * 256] = last(j, grad_block(j)).astype(BF16)

    def norm_block(j):
        return lambda f, r: dot_nt(mm[...], dist[(f * 4 + r) * 2 + (j - 4)])

    i_copies = Copies(i_s, i_r)

    def sum_rows():
        ims[0] = jnp.broadcast_to(jnp.sum(rows_s[...], axis=1, keepdims=True), (ROWS, 128)).T[0:8]
        i_copies.start(ims.at[0], imr.at[0], 0, h_near)

    def sum_pair():
        i_copies.arrived(imr.at[0], 0, h_near)
        ims[1] = ims[0] + imr[0]
        i_copies.start(ims.at[1], imr.at[1], 1, y_up)
        i_copies.start(ims.at[1], imr.at[2], 2, y_down)

    def sum_far():
        i_copies.arrived(imr.at[1], 1, y_down)
        i_copies.arrived(imr.at[2], 2, y_up)
        i_copies.start(imr.at[1], imr.at[3], 3, y_up)

    def sum_all():
        i_copies.arrived(imr.at[3], 3, y_down)
        total = ims[1] + imr[1] + imr[2] + imr[3]
        inner = jnp.broadcast_to(total[0:1], (128, ROWS)).T[:, 0:1] * (1.0 / 4096)
        inner_s[...] = jnp.broadcast_to(inner, (ROWS, 128))

    def stream_grad(j):
        part = j - 4
        column = pl.multiple_of(me * 512 + part * 256, 256)
        gained = (tr.near_last if j in PAIR_FIRST_T else tr.last)(j, norm_block(j)) * gain_ref[:, pl.ds(column, 256)]
        inv = inv_s[:, 0:1]
        scaled = stu[me, :, part * 256 : (part + 1) * 256].astype(F32) * inv
        gs_ref[:, part * 256 : (part + 1) * 256] = inv * (gained - scaled * inner_s[:, 0:1])

    t = [Group(tr, j, (out_block if j < 4 else norm_block)(j), None) for j in range(6)]
    g = [Group(gr, j, grad_block(j), functools.partial(sibling_done, j, False)) for j in range(4)]
    mis = [functools.partial(mismatch, j) for j in range(4)]
    terms = [functools.partial(grad_terms, j) for j in range(4)]
    grad_out = [functools.partial(grad_last, j) for j in range(4)]
    stream_out = [functools.partial(stream_grad, j) for j in (4, 5)]
    near, far, far_pair = (6, 0, True), (15, 2, False), (16, 2, True)
    down, up, down_pair, up_pair = (8, -1, False), (10, 1, False), (12, -1, True), (14, 1, True)

    for task in (
        kvg.own_near, sg.own_ring, kvg.own_across, kvg.own_ring, own_pair, sg.own_near, kvg.got_near,
    ):
        task()
    attended = (
        ((), near),
        ((kvg.up_own, sg.down_own, sg.up_own, dg.own_across, kvg.down_own), up),
        ((kvg.up_pair, kvg.down_pair, dg.own_near), down),
        ((dg.own_ring, kvg.far_own, sg.got_near), up_pair),
        ((), far),
        ((kvg.far_pair,), down_pair),
        ((), far_pair),
    )
    lax.fori_loop(0, 7, step, 0)
    for task in (
        finish_context, t[2].near_first, t[1].first, t[0].first, sg.up_pair, sg.far_own, dg.got_near, dg.down_pair,
        dg.up_pair, t[3].near_first, sg.down_pair, dg.up_own, dg.down_own, t[2].near_ring, t[0].second, dg.far_pair,
        t[2].near_second, dg.far_own, sg.far_pair, normalise, t[1].second, t[0].third, predict_all, t[3].near_ring,
        mis[2], terms[2], t[1].third, t[3].near_second, g[2].first, mis[0], terms[0], mis[1], g[0].first, mis[3],
        t[5].near_first, g[2].second, t[4].first, terms[1], g[1].first, terms[3], g[3].first, sum_rows, g[0].second,
        t[4].second, g[2].third, sum_pair, t[4].third, t[5].near_ring, sum_far, g[1].second, g[0].third, g[3].second,
        sum_all, g[1].third, t[5].near_second, grad_out[2], g[3].third, grad_out[0], stream_out[0], stream_out[1],
        grad_out[1], grad_out[3],
    ):
        task()

    for copies in (kv_copies, d_copies, s_copies, i_copies):
        copies.drain()
    for j in range(4):
        sibling_done(j, True)
    tr.drain()
    gr.drain()


def body(q, k, v, out_proj, teacher_stream, student_stream, gain, distill, mask):
    anywhere = pl.BlockSpec(memory_space=pl.ANY)
    vmem = pl.BlockSpec(memory_space=pltpu.VMEM)
    sem = pltpu.SemaphoreType.DMA
    return pl.pallas_call(
        kernel,
        out_shape=(jax.ShapeDtypeStruct((256, 1024), BF16), jax.ShapeDtypeStruct((ROWS, 512), F32)),
        in_specs=[anywhere] * 6 + [vmem, anywhere, vmem],
        out_specs=(vmem, vmem),
        scratch_shapes=[
            pltpu.VMEM((HEADS, ROWS, HEAD_DIM), BF16),
            pltpu.VMEM((2, 8, 2, ROWS, HEAD_DIM), BF16),
            pltpu.VMEM((16, 256, 1024), BF16),
            pltpu.VMEM((8, ROWS, 512), BF16),
            pltpu.VMEM((ROWS, 4096), BF16),
            pltpu.VMEM((8, 2, 256, ROWS), BF16),
            pltpu.VMEM((4, 8, 2, 256, 256), BF16),
            pltpu.VMEM((3, 7, ROWS, 256), BF16),
            pltpu.VMEM((6, 7, ROWS, 256), BF16),
            pltpu.VMEM((2, 7, 256, 256), BF16),
            pltpu.VMEM((4, 7, 256, 256), BF16),
            pltpu.VMEM((4, 8, 256, 256), BF16),
            pltpu.VMEM((4, ROWS, 256), F32),
            pltpu.VMEM((ROWS, 1024), BF16),
            pltpu.VMEM((ROWS, 1024), BF16),
            pltpu.VMEM((ROWS, 128), F32),
            pltpu.VMEM((HEADS, ROWS, 2 * HEAD_DIM), F32),
            pltpu.VMEM((HEADS, ROWS, 128), F32),
            pltpu.VMEM((ROWS, 512), BF16),
            pltpu.VMEM((ROWS, 128), F32),
            pltpu.VMEM((ROWS, 128), F32),
            pltpu.VMEM((ROWS, 128), F32),
            pltpu.VMEM((2, 8, ROWS), F32),
            pltpu.VMEM((4, 8, ROWS), F32),
            sem((9,)), sem((4, 8, 2)),
            sem((17,)), sem((17,)), sem((17,)), sem((17,)), sem((17,)), sem((17,)),
            sem((48,)), sem((48,)), sem((32,)), sem((32,)), sem((4,)), sem((4,)), sem((4,)), sem((4,)),
        ],
        compiler_params=pltpu.CompilerParams(
            collective_id=0, has_side_effects=True, vmem_limit_bytes=65400 * 1024
        ),
        name="distill",
    )(
        q, k, v, out_proj, teacher_stream, student_stream, gain.reshape(1, 4096), distill,
        mask.reshape(3, 128),
    )


def solution(mesh):
    placed = (
        P("seq", "tensor"),
        P("seq", "tensor"),
        P("seq", "tensor"),
        P("tensor", None),
        P("seq", "tensor"),
        P("seq", "tensor"),
        P(),
        P("seq", "tensor"),
        P("seq"),
    )
    return jax.shard_map(
        body,
        mesh=mesh,
        in_specs=placed,
        out_specs=(P("seq", "tensor"), P("seq", "tensor")),
        check_vma=False,
    )
```

```python
import functools
import math

import jax
import jax.numpy as jnp
from jax import lax
from jax.experimental import pallas as pl
from jax.experimental.pallas import tpu as pltpu
from jax.sharding import PartitionSpec as P

HEADS = 4
HEAD_DIM = 128
EPS = 1e-05
ROWS = 384
MASKED = -1e30
MESH = pl.DeviceIdType.MESH
F32 = jnp.float32
BF16 = jnp.bfloat16


def dot(a, b):
    return jnp.dot(a, b, preferred_element_type=F32)


def dot_nt(a, b):
    return lax.dot_general(a, b, (((1,), (1,)), ((), ())), preferred_element_type=F32)


PAIR_FIRST_T = (2, 3, 5)
PAIR_FIRST_G = ()


class Copies:
    def __init__(self, send, recv):
        self.send, self.recv = send, recv
        self.started = []

    def make(self, src, dst, k, device):
        return pltpu.make_async_remote_copy(
            src_ref=src, dst_ref=dst, send_sem=self.send.at[k], recv_sem=self.recv.at[k],
            device_id=device, device_id_type=MESH,
        )

    def start(self, src, dst, k, device, again=None):
        self.make(src, dst, k, device).start()
        self.started.append((again or (lambda: src), k, device))

    def arrived(self, ref, k, device):
        self.make(ref, ref, k, device).wait_recv()

    def drain(self):
        for again, k, device in self.started:
            src = again()
            self.make(src, src, k, device).wait_send()
        self.started = []


class Gather:
    def __init__(self, copies, whole, half, near, up, down, ring, pair, other):
        self.c, self.whole, self.half = copies, whole, half
        self.near, self.up, self.down = near, up, down
        self.ring, self.pair, self.other = ring, pair, other
        self.loads = []

    def loaded(self):
        for copy in self.loads:
            copy.wait()
        self.loads = []

    def at(self, turn, flip):
        r = lax.rem(self.ring + (turn + 4), 4)
        f = 1 - self.pair if flip else self.pair
        return r, f

    def go(self, k, device, place):
        ref = self.whole(*self.at(*place))
        self.c.start(ref, ref, k, device, lambda: self.whole(*self.at(*place)))

    def go_half(self, k, device, place, part):
        ref = self.half(*self.at(*place), part)
        self.c.start(ref, ref, k, device, lambda: self.half(*self.at(*place), part))

    def across(self, k, place):
        if self.other is not None:
            self.go(k, self.other, place)

    def own_near(self):
        self.loaded()
        self.go(0, self.near, (0, False))

    def own_ring(self):
        self.loaded()
        self.go(1, self.up, (0, False))
        self.go(2, self.down, (0, False))

    def own_across(self):
        self.loaded()
        self.across(3, (0, False))

    def got_near(self):
        place = (0, True)
        self.c.arrived(self.whole(*self.at(*place)), 0, self.near)
        self.go(4, self.up, place)
        self.go(5, self.down, place)
        self.across(6, place)

    def got_from_down(self, flip):
        place = (-1, flip)
        self.c.arrived(self.whole(*self.at(*place)), 4 if flip else 1, self.down)
        self.go_half(11 if flip else 7, self.up, place, 0)
        self.across(12 if flip else 8, place)

    def got_from_up(self, flip):
        place = (1, flip)
        self.c.arrived(self.whole(*self.at(*place)), 5 if flip else 2, self.up)
        self.go_half(13 if flip else 9, self.down, place, 1)
        self.across(14 if flip else 10, place)

    def got_far(self, flip):
        place = (2, flip)
        self.c.arrived(self.half(*self.at(*place), 0), 11 if flip else 7, self.down)
        self.c.arrived(self.half(*self.at(*place), 1), 13 if flip else 9, self.up)
        self.across(16 if flip else 15, place)

    def down_own(self):
        self.got_from_down(False)

    def down_pair(self):
        self.got_from_down(True)

    def up_own(self):
        self.got_from_up(False)

    def up_pair(self):
        self.got_from_up(True)

    def far_own(self):
        self.got_far(False)

    def far_pair(self):
        self.got_far(True)


class Reduce:
    def __init__(self, copies, out, got, near, up, down, ring, pair, places):
        self.c, self.out, self.got = copies, out, got
        self.near, self.up, self.down = near, up, down
        self.ring, self.pair, self.places = ring, pair, places
        self.half = out.shape[2] // 2
        self.pending = {}

    def to(self, turn):
        return lax.rem(self.ring + (turn + 4), 4)

    def put(self, j, slot, value):
        o = self.places[j]
        for src, sem, device in self.pending.pop((o, slot), []):
            self.c.make(src, src, sem, device).wait_send()
        self.out[o, slot] = value.astype(BF16)

    def post(self, j, slot, k, device, part=None):
        rows = slice(None) if part is None else pl.ds(part * self.half, self.half)
        o, sem = self.places[j], j * 8 + k
        src = self.out.at[o, slot, rows]
        self.c.make(src, self.got.at[j, slot, rows], sem, device).start()
        self.pending.setdefault((o, slot), []).append((src, sem, device))

    def send(self, j, k, device, value):
        self.put(j, k, value)
        self.post(j, k, k, device)

    def arrived(self, j, slot, k, device, part=None):
        rows = slice(None) if part is None else pl.ds(part * self.half, self.half)
        ref = self.got.at[j, slot, rows]
        self.c.make(ref, ref, j * 8 + k, device).wait_recv()

    def load(self, j, k):
        return self.got[j, k].astype(F32)


    def first(self, j, block):
        self.send(j, 0, self.up, block(0, self.to(2)))
        self.send(j, 1, self.down, block(1, self.to(2)))
        self.send(j, 2, self.up, block(1, self.to(1)))
        self.send(j, 3, self.down, block(0, self.to(-1)))

    def second(self, j, block):
        self.arrived(j, 0, 0, self.down)
        self.send(j, 4, self.up, block(0, self.to(1)) + self.load(j, 0))
        self.arrived(j, 1, 1, self.up)
        self.send(j, 5, self.down, block(1, self.to(-1)) + self.load(j, 1))

    def total(self, j, block, f):
        return block(f, self.ring) + self.load(j, 4 - 2 * f) + self.load(j, 3 + 2 * f)

    def third(self, j, block):
        for k, device in ((2, self.down), (3, self.up), (4, self.down), (5, self.up)):
            self.arrived(j, k, k, device)
        self.send(j, 6, self.near, self.total(j, block, 1 - self.pair))

    def last(self, j, block):
        mine = self.total(j, block, self.pair)
        self.arrived(j, 6, 6, self.near)
        return mine + self.load(j, 6)


    def near_first(self, j, block):
        for r in range(4):
            self.send(j, r, self.near, block(1 - self.pair, r))

    def both(self, j, block, r):
        return block(self.pair, r) + self.load(j, r)

    def near_ring(self, j, block):
        for r in range(4):
            self.arrived(j, r, r, self.near)
        self.put(j, 4, self.both(j, block, self.to(2)))
        self.post(j, 4, 4, self.up, 0)
        self.post(j, 4, 5, self.down, 1)

    def near_second(self, j, block):
        o, n = self.places[j], self.half
        value = self.both(j, block, self.to(1))
        self.arrived(j, 4, 4, self.down, 0)
        self.put(j, 5, value)
        self.out[o, 5, 0:n] = (value[0:n] + self.got[j, 4, 0:n].astype(F32)).astype(BF16)
        self.post(j, 5, 6, self.up)
        value = self.both(j, block, self.to(-1))
        self.arrived(j, 4, 5, self.up, 1)
        self.put(j, 6, value)
        self.out[o, 6, n : 2 * n] = (value[n : 2 * n] + self.got[j, 4, n : 2 * n].astype(F32)).astype(BF16)
        self.post(j, 6, 7, self.down)

    def near_last(self, j, block):
        mine = self.both(j, block, self.ring)
        self.arrived(j, 5, 6, self.down)
        self.arrived(j, 6, 7, self.up)
        return mine + self.load(j, 5) + self.load(j, 6)

    def drain(self):
        for sent in self.pending.values():
            for src, sem, device in sent:
                self.c.make(src, src, sem, device).wait_send()
        self.pending = {}


class Group:
    def __init__(self, reduce, j, block, ready):
        self.reduce, self.j, self.block, self.ready = reduce, j, block, ready

    def first(self):
        if self.ready is not None:
            self.ready()
        self.reduce.first(self.j, self.block)

    def near_first(self):
        if self.ready is not None:
            self.ready()
        self.reduce.near_first(self.j, self.block)

    def second(self):
        self.reduce.second(self.j, self.block)

    def third(self):
        self.reduce.third(self.j, self.block)

    def near_ring(self):
        self.reduce.near_ring(self.j, self.block)

    def near_second(self):
        self.reduce.near_second(self.j, self.block)


def kernel(
    q_hbm, k_hbm, v_hbm, op_hbm, ts_hbm, ss_hbm, gain_ref, dp_hbm, mask_ref,
    gd_ref, gs_ref,
    q4, kv, dist, stu, normed, normed_t, big, tout, tgot, gout, ggot, sib,
    pred, mm, ts_ref, mask_s, acc, m_s, ctx, inv_s, rows_s, inner_s, ims, imr,
    local, op_sem, kv_s, kv_r, d_s, d_r, s_s, s_r, t_s, t_r, g_s, g_r, b_s, b_r, i_s, i_r,
):
    me, s = lax.axis_index("tensor"), lax.axis_index("seq")
    h, y = lax.div(me, 4), lax.rem(me, 4)
    z, x, c = lax.div(s, 4), lax.rem(lax.div(s, 2), 2), lax.rem(s, 2)
    p = lax.div(s, 2)

    def on_seq(zz, xx, cc):
        return {"tensor": me, "seq": zz * 4 + xx * 2 + cc}

    def on_tensor(hh, yy):
        return {"tensor": hh * 4 + yy, "seq": s}

    z_up, z_down = on_seq(lax.rem(z + 1, 4), x, c), on_seq(lax.rem(z + 3, 4), x, c)
    x_near, sibling = on_seq(z, 1 - x, c), on_seq(z, x, 1 - c)
    y_up, y_down = on_tensor(h, lax.rem(y + 1, 4)), on_tensor(h, lax.rem(y + 3, 4))
    h_near = on_tensor(1 - h, y)

    own_copies = [
        pltpu.make_async_copy(k_hbm, kv.at[0, p, c], local.at[0]),
        pltpu.make_async_copy(v_hbm, kv.at[1, p, c], local.at[1]),
        pltpu.make_async_copy(ss_hbm, stu.at[me], local.at[2]),
        pltpu.make_async_copy(dp_hbm, dist.at[s], local.at[3]),
    ] + [
        pltpu.make_async_copy(q_hbm.at[:, pl.ds(i * HEAD_DIM, HEAD_DIM)], q4.at[i], local.at[4 + i])
        for i in range(HEADS)
    ]
    for copy in own_copies:
        copy.start()

    barrier = pltpu.get_barrier_semaphore()
    for device in (z_up, z_down, x_near, sibling, y_up, y_down, h_near):
        pl.semaphore_signal(barrier, inc=1, device_id=device, device_id_type=MESH)
    pl.semaphore_wait(barrier, 7)

    kv_copies, d_copies, s_copies = Copies(kv_s, kv_r), Copies(d_s, d_r), Copies(s_s, s_r)

    def kv_gather(core):
        return Gather(
            kv_copies, lambda r, f: kv.at[:, r * 2 + f, core], lambda r, f, part: kv.at[part, r * 2 + f, core],
            x_near, z_up, z_down, z, x, sibling,
        )

    def d_gather(core):
        return Gather(
            d_copies, lambda r, f: dist.at[(r * 2 + f) * 2 + core],
            lambda r, f, part: dist.at[(r * 2 + f) * 2 + core, pl.ds(part * 128, 128)],
            x_near, z_up, z_down, z, x, sibling,
        )

    kvg, dg = kv_gather(c), d_gather(c)
    sg = Gather(
        s_copies, lambda r, f: stu.at[f * 4 + r],
        lambda r, f, part: stu.at[f * 4 + r, pl.ds(part * 192, 192)],
        h_near, y_up, y_down, y, h, None,
    )

    def from_sibling(gather, copies, k, turn, flip):
        copies.arrived(gather.whole(*gather.at(turn, flip)), k, sibling)

    kv_other, d_other = kv_gather(1 - c), d_gather(1 - c)

    kvg.loads, sg.loads, dg.loads = own_copies[0:2], own_copies[2:3], own_copies[3:4]

    def weight_copy(j, i):
        start = pl.multiple_of(i * 1024 + j * 256, 256)
        return pltpu.make_async_copy(op_hbm.at[:, :, pl.ds(start, 256)], big.at[j, i], op_sem.at[j, i])

    def load_out_proj(i, carry):
        for j in range(4):
            weight_copy(j, i).start()
        return carry

    load_stream = pltpu.make_async_copy(ts_hbm, ts_ref, local.at[8])

    def load_later():
        lax.fori_loop(0, 8, load_out_proj, 0)
        load_stream.start()
        rows_s[...] = jnp.zeros_like(rows_s)

    scale = math.log2(math.e) / math.sqrt(HEAD_DIM)

    ones = jnp.ones((2 * ROWS, HEAD_DIM), BF16)

    def keys_values(block):
        values = kv[1, block].reshape(2 * ROWS, HEAD_DIM)
        return kv[0, block].reshape(2 * ROWS, HEAD_DIM), jnp.concatenate([values, ones], axis=1)

    def own_pair():
        for copy in own_copies[4:]:
            copy.wait()
        from_sibling(kv_other, kv_copies, 3, 0, False)
        keys, values = keys_values(p)
        visible = (
            lax.broadcasted_iota(jnp.int32, (ROWS, 2 * ROWS), 1)
            <= lax.broadcasted_iota(jnp.int32, (ROWS, 2 * ROWS), 0) + c * ROWS
        )
        scores = dot_nt(q4[0], keys)
        for i in range(HEADS):
            following = dot_nt(q4[i + 1], keys) if i + 1 < HEADS else None
            scores = jnp.where(visible, scores * scale, MASKED)
            top = jnp.max(scores, axis=1, keepdims=True)
            weights = jnp.exp2(scores - top)
            m_s[i] = jnp.broadcast_to(top, (ROWS, 128))
            acc[i] = dot(weights.astype(BF16), values)
            scores = following
        load_later()

    def step(i, carry):
        turn, flip = 0, 0
        for k, (tasks, (copy, turn_k, flip_k)) in enumerate(attended):
            @pl.when(i == k)
            def _(tasks=tasks, copy=copy, turn_k=turn_k, flip_k=flip_k):
                for task in tasks:
                    task()
                from_sibling(kv_other, kv_copies, copy, turn_k, flip_k)

            turn = jnp.where(i == k, turn_k % 4, turn)
            flip = jnp.where(i == k, int(flip_k), flip)
        block = lax.rem(z + turn, 4) * 2 + x * (1 - flip) + (1 - x) * flip

        @pl.when(block < p)
        def _():
            keys, values = keys_values(block)
            scores = dot_nt(q4[0], keys)
            for i in range(HEADS):
                following = dot_nt(q4[i + 1], keys) if i + 1 < HEADS else None
                before = m_s[i, :, 0:1]
                top = jnp.maximum(before, jnp.max(scores, axis=1, keepdims=True) * scale)
                weights = jnp.exp2(scores * scale - top)
                m_s[i] = jnp.broadcast_to(top, (ROWS, 128))
                acc[i] = acc[i] * jnp.exp2(before - top) + dot(weights.astype(BF16), values)
                scores = following

        return carry

    t_copies, g_copies = Copies(t_s, t_r), Copies(g_s, g_r)
    tr = Reduce(t_copies, tout, tgot, h_near, y_up, y_down, y, h, (0, 1, 2, 0, 1, 2))
    gr = Reduce(g_copies, gout, ggot, x_near, z_up, z_down, z, x, (0, 1, 0, 1))

    def out_block(j):
        return lambda f, r: dot(ctx[...], big[j, f * 4 + r].reshape(512, 256))

    def out_proj_here(j):
        def wait(i, carry):
            weight_copy(j, i).wait()
            return carry

        lax.fori_loop(0, 8, wait, 0)

    def finish_context():
        for i in range(HEADS):
            ctx[:, i * HEAD_DIM : (i + 1) * HEAD_DIM] = (acc[i, :, 0:HEAD_DIM] / acc[i, :, HEAD_DIM:]).astype(BF16)
        for j in range(4):
            out_proj_here(j)
        load_stream.wait()
        for i in range(3):
            row = mask_ref[i : i + 1, :].astype(F32)
            mask_s[i * 128 : (i + 1) * 128, :] = jnp.broadcast_to(row, (128, 128)).T

    def squares(i, total):
        block = stu[i].astype(F32)
        block = block * block
        return total + block[:, 0:128] + block[:, 128:256] + block[:, 256:384] + block[:, 384:512]

    def make_normed(i, carry):
        column = pl.multiple_of(i * 512, 512)
        rows = (stu[i].astype(F32) * inv_s[:, 0:1]) * gain_ref[:, pl.ds(column, 512)]
        normed[:, pl.ds(column, 512)] = rows.astype(BF16)
        normed_t[i, 0] = rows[:, 0:256].T.astype(BF16)
        normed_t[i, 1] = rows[:, 256:512].T.astype(BF16)
        return carry

    def normalise():
        square_sum = lax.fori_loop(0, 8, squares, jnp.zeros((ROWS, 128), F32))
        inverse = lax.rsqrt(jnp.sum(square_sum, axis=1, keepdims=True) * (1.0 / 4096) + EPS)
        inv_s[...] = jnp.broadcast_to(inverse, (ROWS, 128))
        lax.fori_loop(0, 8, make_normed, 0)

    def predict(j, carry):
        pred[j] = dot(normed[...], dist[:, :, pl.ds(pl.multiple_of(j * 256, 256), 256)].reshape(4096, 256))
        return carry

    def predict_all():
        for k, turn, flip in (
            (3, 0, 0), (6, 0, 1), (8, -1, 0), (10, 1, 0), (12, -1, 1), (14, 1, 1), (15, 2, 0), (16, 2, 1)
        ):
            from_sibling(d_other, d_copies, k, turn, flip)
        lax.fori_loop(0, 4, predict, 0)

    inv_scale = 1.0 / math.sqrt(16 * ROWS)

    def mismatch(j):
        teacher = (tr.near_last if j in PAIR_FIRST_T else tr.last)(j, out_block(j))
        target = (ts_ref[:, j * 256 : (j + 1) * 256].astype(F32) + teacher).astype(BF16).astype(F32)
        half = (mask_s[:, 0:1] * (pred[j] - target)).astype(BF16)
        mm[:, j * 256 : (j + 1) * 256] = half
        product = half.astype(F32) * pred[j]
        rows = product[:, 0:128] + product[:, 128:256]
        rows_s[...] = rows_s[...] + rows

    def grad_terms(j):
        mine = mm[:, j * 256 : (j + 1) * 256]

        def term(core):
            rows = normed_t[:, core].reshape(2048, ROWS)
            big[j, :, core] = (dot(rows, mine) * inv_scale).astype(BF16).reshape(8, 256, 256)

        term(1 - c)
        src = big.at[j, :, 1 - c]
        pltpu.make_async_remote_copy(
            src_ref=src, dst_ref=sib.at[j], send_sem=b_s.at[j], recv_sem=b_r.at[j],
            device_id=sibling, device_id_type=MESH,
        ).start()
        term(c)

    def sibling_done(j, send):
        src = big.at[j, :, 1 - c]
        copy = pltpu.make_async_remote_copy(
            src_ref=src, dst_ref=sib.at[j], send_sem=b_s.at[j], recv_sem=b_r.at[j],
            device_id=sibling, device_id_type=MESH,
        )
        if send:
            copy.wait_send()
        else:
            copy.wait_recv()

    def grad_block(j):
        return lambda f, r: big[j, r * 2 + f, c].astype(F32) + sib[j, r * 2 + f].astype(F32)

    def grad_last(j):
        last = gr.near_last if j in PAIR_FIRST_G else gr.last
        gd_ref[:, j * 256 : (j + 1) * 256] = last(j, grad_block(j)).astype(BF16)

    def norm_block(j):
        return lambda f, r: dot_nt(mm[...], dist[(f * 4 + r) * 2 + (j - 4)])

    i_copies = Copies(i_s, i_r)

    def sum_rows():
        ims[0] = jnp.broadcast_to(jnp.sum(rows_s[...], axis=1, keepdims=True), (ROWS, 128)).T[0:8]
        i_copies.start(ims.at[0], imr.at[0], 0, h_near)

    def sum_pair():
        i_copies.arrived(imr.at[0], 0, h_near)
        ims[1] = ims[0] + imr[0]
        i_copies.start(ims.at[1], imr.at[1], 1, y_up)
        i_copies.start(ims.at[1], imr.at[2], 2, y_down)

    def sum_far():
        i_copies.arrived(imr.at[1], 1, y_down)
        i_copies.arrived(imr.at[2], 2, y_up)
        i_copies.start(imr.at[1], imr.at[3], 3, y_up)

    def sum_all():
        i_copies.arrived(imr.at[3], 3, y_down)
        total = ims[1] + imr[1] + imr[2] + imr[3]
        inner = jnp.broadcast_to(total[0:1], (128, ROWS)).T[:, 0:1] * (1.0 / 4096)
        inner_s[...] = jnp.broadcast_to(inner, (ROWS, 128))

    def stream_grad(j):
        part = j - 4
        column = pl.multiple_of(me * 512 + part * 256, 256)
        gained = (tr.near_last if j in PAIR_FIRST_T else tr.last)(j, norm_block(j)) * gain_ref[:, pl.ds(column, 256)]
        inv = inv_s[:, 0:1]
        scaled = stu[me, :, part * 256 : (part + 1) * 256].astype(F32) * inv
        gs_ref[:, part * 256 : (part + 1) * 256] = inv * (gained - scaled * inner_s[:, 0:1])

    t = [Group(tr, j, (out_block if j < 4 else norm_block)(j), None) for j in range(6)]
    g = [Group(gr, j, grad_block(j), functools.partial(sibling_done, j, False)) for j in range(4)]
    mis = [functools.partial(mismatch, j) for j in range(4)]
    terms = [functools.partial(grad_terms, j) for j in range(4)]
    grad_out = [functools.partial(grad_last, j) for j in range(4)]
    stream_out = [functools.partial(stream_grad, j) for j in (4, 5)]
    near, far, far_pair = (6, 0, True), (15, 2, False), (16, 2, True)
    down, up, down_pair, up_pair = (8, -1, False), (10, 1, False), (12, -1, True), (14, 1, True)

    for task in (
        kvg.own_near, sg.own_ring, kvg.own_across, kvg.own_ring, own_pair, sg.own_near, kvg.got_near,
    ):
        task()
    attended = (
        ((), near),
        ((kvg.up_own, sg.down_own, sg.up_own, dg.own_across, kvg.down_own), up),
        ((kvg.up_pair, kvg.down_pair, dg.own_near), down),
        ((dg.own_ring, kvg.far_own, sg.got_near), up_pair),
        ((), far),
        ((kvg.far_pair,), down_pair),
        ((), far_pair),
    )
    lax.fori_loop(0, 7, step, 0)
    for task in (
        finish_context, t[2].near_first, t[1].first, t[0].first, sg.up_pair, sg.far_own, dg.got_near, dg.down_pair,
        dg.up_pair, t[3].near_first, sg.down_pair, dg.up_own, dg.down_own, t[2].near_ring, t[0].second, dg.far_pair,
        t[2].near_second, dg.far_own, sg.far_pair, normalise, t[1].second, t[0].third, predict_all, t[3].near_ring,
        mis[2], terms[2], t[1].third, t[3].near_second, g[2].first, mis[0], terms[0], mis[1], g[0].first, mis[3],
        t[5].near_first, g[2].second, t[4].first, terms[1], g[1].first, terms[3], g[3].first, sum_rows, g[0].second,
        t[4].second, g[2].third, sum_pair, t[4].third, t[5].near_ring, sum_far, g[1].second, g[0].third, g[3].second,
        sum_all, g[1].third, t[5].near_second, grad_out[2], g[3].third, grad_out[0], stream_out[0], stream_out[1],
        grad_out[1], grad_out[3],
    ):
        task()

    for copies in (kv_copies, d_copies, s_copies, i_copies):
        copies.drain()
    for j in range(4):
        sibling_done(j, True)
    tr.drain()
    gr.drain()


def body(q, k, v, out_proj, teacher_stream, student_stream, gain, distill, mask):
    anywhere = pl.BlockSpec(memory_space=pl.ANY)
    vmem = pl.BlockSpec(memory_space=pltpu.VMEM)
    sem = pltpu.SemaphoreType.DMA
    return pl.pallas_call(
        kernel,
        out_shape=(jax.ShapeDtypeStruct((256, 1024), BF16), jax.ShapeDtypeStruct((ROWS, 512), F32)),
        in_specs=[anywhere] * 6 + [vmem, anywhere, vmem],
        out_specs=(vmem, vmem),
        scratch_shapes=[
            pltpu.VMEM((HEADS, ROWS, HEAD_DIM), BF16),
            pltpu.VMEM((2, 8, 2, ROWS, HEAD_DIM), BF16),
            pltpu.VMEM((16, 256, 1024), BF16),
            pltpu.VMEM((8, ROWS, 512), BF16),
            pltpu.VMEM((ROWS, 4096), BF16),
            pltpu.VMEM((8, 2, 256, ROWS), BF16),
            pltpu.VMEM((4, 8, 2, 256, 256), BF16),
            pltpu.VMEM((3, 7, ROWS, 256), BF16),
            pltpu.VMEM((6, 7, ROWS, 256), BF16),
            pltpu.VMEM((2, 7, 256, 256), BF16),
            pltpu.VMEM((4, 7, 256, 256), BF16),
            pltpu.VMEM((4, 8, 256, 256), BF16),
            pltpu.VMEM((4, ROWS, 256), F32),
            pltpu.VMEM((ROWS, 1024), BF16),
            pltpu.VMEM((ROWS, 1024), BF16),
            pltpu.VMEM((ROWS, 128), F32),
            pltpu.VMEM((HEADS, ROWS, 2 * HEAD_DIM), F32),
            pltpu.VMEM((HEADS, ROWS, 128), F32),
            pltpu.VMEM((ROWS, 512), BF16),
            pltpu.VMEM((ROWS, 128), F32),
            pltpu.VMEM((ROWS, 128), F32),
            pltpu.VMEM((ROWS, 128), F32),
            pltpu.VMEM((2, 8, ROWS), F32),
            pltpu.VMEM((4, 8, ROWS), F32),
            sem((9,)), sem((4, 8)),
            sem((17,)), sem((17,)), sem((17,)), sem((17,)), sem((17,)), sem((17,)),
            sem((48,)), sem((48,)), sem((32,)), sem((32,)), sem((4,)), sem((4,)), sem((4,)), sem((4,)),
        ],
        compiler_params=pltpu.CompilerParams(
            collective_id=0, has_side_effects=True, vmem_limit_bytes=65400 * 1024
        ),
        name="distill",
    )(
        q, k, v, out_proj.reshape(2, 256, 8192), teacher_stream, student_stream, gain.reshape(1, 4096), distill,
        mask.reshape(3, 128),
    )


def solution(mesh):
    placed = (
        P("seq", "tensor"),
        P("seq", "tensor"),
        P("seq", "tensor"),
        P("tensor", None),
        P("seq", "tensor"),
        P("seq", "tensor"),
        P(),
        P("seq", "tensor"),
        P("seq"),
    )
    return jax.shard_map(
        body,
        mesh=mesh,
        in_specs=placed,
        out_specs=(P("seq", "tensor"), P("seq", "tensor")),
        check_vma=False,
    )
```
